32 devices in a mesh: ctx: 16 (over z, y, core), head: 2 (over x).
Axes of the slice: x: 2, y: 2, z: 4, core: 2. Of those that a mesh axis runs over, the one named last changes fastest.
Arguments:
- queries: bfloat16 [1024, 2048], P('ctx', 'head'), may hold values from -6 to 6
- keys_first: bfloat16 [1024, 512], P('ctx', 'head'), may hold values from -6 to 6
- primary_value_array: bfloat16 [1024, 512], P('ctx', 'head'), may hold values from -6 to 6
- keys_second: bfloat16 [1024, 512], P('ctx', 'head'), may hold values from -6 to 6
- secondary_value_array: bfloat16 [1024, 512], P('ctx', 'head'), may hold values from -6 to 6
- out_weight: bfloat16 [2048, 4096], P('head'), may hold values from -6 to 6
Outputs:
- projected: bfloat16 [1024, 4096], P('ctx', 'head')
The draws below stay inside these ranges and needn't reach their ends.
All inputs are finite; a program needn't handle non-finite values.
Results may differ from the reference program's by a relative error of at most 0.01.
Values may be sent and summed in bfloat16 or wider, within the bound.
A program may use at most 128 MiB of HBM per device.

```python
import math
import jax
import jax.numpy as jnp
from jax import lax

D = 4096
QUERY_HEADS = 16
KEY_VALUE_HEADS = 4
HEAD_SIZE = 128
FIRST_WINDOW = 512
SECOND_WINDOW = 16
TOKENS_PER_SHARE = 64
TOKEN_COUNT = 1024


def draw_queries(key, part):
    final_output = jax.random.truncated_normal(jax.random.fold_in(key, 11), -6.0, 6.0, (TOKEN_COUNT, QUERY_HEADS * HEAD_SIZE), jnp.float32)
    return final_output.astype(jnp.bfloat16)


def draw_keys_first(key, part):
    final_output = jax.random.truncated_normal(jax.random.fold_in(key, 12), -6.0, 6.0, (TOKEN_COUNT, KEY_VALUE_HEADS * HEAD_SIZE), jnp.float32)
    return final_output.astype(jnp.bfloat16)


def draw_keys_second(key, part):
    final_output = jax.random.truncated_normal(jax.random.fold_in(key, 13), -6.0, 6.0, (TOKEN_COUNT, KEY_VALUE_HEADS * HEAD_SIZE), jnp.float32)
    return final_output.astype(jnp.bfloat16)


def shard_levels(own_key, extent, split, low, top_value):
    level, own = 1.0, jax.random.fold_in(own_key, 6)
    for position, blocks in split:
        steps = jnp.exp(jax.random.uniform(jax.random.fold_in(own, position), (blocks,), jnp.float32, low / len(split), top_value / len(split)))
        level = level * jnp.repeat(steps, extent[position] // blocks).reshape([-1 if axis == position else 1 for axis in range(len(extent))])
    return level


def centred(own_key, shape, width, most, pieces=(), kind=jnp.bfloat16):
    values = jax.random.normal(own_key, shape, jnp.float32) * width
    if len(pieces) > 0:
        values = shard_levels(own_key, shape, pieces, -0.22, 0.18) * values
    return jnp.clip(values, min=-most, max=most).astype(kind)


def setup_inputs(seed: int = 0) -> dict:
    arg_keys = jax.random.split(jax.random.key(seed), 7)
    return {
        "queries": draw_queries(jax.random.fold_in(arg_keys[6], 71), 0),
        "keys_first": draw_keys_first(jax.random.fold_in(arg_keys[6], 71), 0),
        "primary_value_array": centred(arg_keys[2], (TOKEN_COUNT, KEY_VALUE_HEADS * HEAD_SIZE), 1.0, 6.0, ((0, 16), (1, 2))),
        "keys_second": draw_keys_second(jax.random.fold_in(arg_keys[6], 71), 0),
        "secondary_value_array": centred(arg_keys[4], (TOKEN_COUNT, KEY_VALUE_HEADS * HEAD_SIZE), 1.0, 6.0, ((0, 16), (1, 2))),
        "out_weight": centred(arg_keys[5], (QUERY_HEADS * HEAD_SIZE, D), 1.0, 6.0, ((0, 2),)),
    }


NEGATIVE = -1e+30

def reference(queries, keys_first, primary_value_array, keys_second, secondary_value_array, out_weight):
    group_count = QUERY_HEADS // KEY_VALUE_HEADS
    score_scale = 1.0 / math.sqrt(HEAD_SIZE)
    column_span = KEY_VALUE_HEADS * HEAD_SIZE
    padded_keys = jnp.concatenate([jnp.zeros((FIRST_WINDOW, column_span), keys_first.dtype), keys_first], axis=0)
    padded_values = jnp.concatenate([jnp.zeros((FIRST_WINDOW, column_span), primary_value_array.dtype), primary_value_array], axis=0)
    padded_second = jnp.concatenate([jnp.zeros((SECOND_WINDOW, column_span), keys_second.dtype), keys_second], axis=0)
    padded_svalues = jnp.concatenate([jnp.zeros((SECOND_WINDOW, column_span), secondary_value_array.dtype), secondary_value_array], axis=0)

    def one_block(block_index):
        block_start = (block_index * TOKENS_PER_SHARE).astype(jnp.int32)
        rows_of_query = lax.dynamic_slice_in_dim(queries, block_start, TOKENS_PER_SHARE, 0)
        primary_keys = lax.dynamic_slice_in_dim(padded_keys, block_start, FIRST_WINDOW + TOKENS_PER_SHARE, 0)
        primary_values = lax.dynamic_slice_in_dim(padded_values, block_start, FIRST_WINDOW + TOKENS_PER_SHARE, 0)
        second_slab = lax.dynamic_slice_in_dim(padded_second, block_start + 1, TOKENS_PER_SHARE + SECOND_WINDOW - 1, 0)
        svalue_slab = lax.dynamic_slice_in_dim(padded_svalues, block_start + 1, TOKENS_PER_SHARE + SECOND_WINDOW - 1, 0)
        secondary_keys = jnp.stack([second_slab[offset:offset + TOKENS_PER_SHARE] for offset in range(SECOND_WINDOW)], axis=1)
        secondary_values = jnp.stack([svalue_slab[offset:offset + TOKENS_PER_SHARE] for offset in range(SECOND_WINDOW)], axis=1)
        head_queries = rows_of_query.astype(jnp.float32).reshape(TOKENS_PER_SHARE, KEY_VALUE_HEADS, group_count, HEAD_SIZE).transpose(1, 2, 0, 3)[:, :, :, None, :]
        secondary_heads = secondary_keys.astype(jnp.float32).reshape(TOKENS_PER_SHARE, SECOND_WINDOW, KEY_VALUE_HEADS, HEAD_SIZE).transpose(2, 0, 1, 3)[:, None]
        secondary_value_heads = secondary_values.astype(jnp.float32).reshape(TOKENS_PER_SHARE, SECOND_WINDOW, KEY_VALUE_HEADS, HEAD_SIZE).transpose(2, 0, 1, 3)[:, None]
        products = (head_queries * secondary_heads * score_scale).astype(jnp.bfloat16)
        products = lax.optimization_barrier(products).astype(jnp.float32)
        head_keys = primary_keys.astype(jnp.float32).reshape(FIRST_WINDOW + TOKENS_PER_SHARE, KEY_VALUE_HEADS, HEAD_SIZE)
        head_values = primary_values.astype(jnp.float32).reshape(FIRST_WINDOW + TOKENS_PER_SHARE, KEY_VALUE_HEADS, HEAD_SIZE)
        scores = jnp.einsum('gmtod,jgd->gmjto', products, head_keys, precision=lax.Precision.HIGHEST)
        key_pos = block_start - FIRST_WINDOW + jnp.arange(FIRST_WINDOW + TOKENS_PER_SHARE, dtype=jnp.int32)
        query_pos = block_start + jnp.arange(TOKENS_PER_SHARE, dtype=jnp.int32)
        second_pos = query_pos[:, None] - SECOND_WINDOW + 1 + jnp.arange(SECOND_WINDOW, dtype=jnp.int32)[None, :]
        allowed_pairs = (key_pos[:, None] <= query_pos[None, :]) & (key_pos[:, None] > query_pos[None, :] - FIRST_WINDOW) & (key_pos[:, None] >= 0)
        allowed_pairs = allowed_pairs[:, :, None] & (second_pos >= 0)[None]
        masked = jnp.where(allowed_pairs, scores, NEGATIVE)
        row_top = lax.optimization_barrier(jnp.max(masked, axis=(2, 4), keepdims=True))
        expo = jnp.where(allowed_pairs, jnp.exp(scores - row_top), 0.0)
        row_total = lax.optimization_barrier(jnp.sum(expo, axis=(2, 4)))
        weights = lax.optimization_barrier(expo.astype(jnp.bfloat16)).astype(jnp.float32)
        mixture = jnp.einsum('gmjto,jgd->gmtod', weights, head_values, precision=lax.Precision.HIGHEST)
        attention = lax.optimization_barrier(jnp.sum(mixture * secondary_value_heads, axis=3)) / row_total[..., None]
        return attention.transpose(2, 0, 1, 3).reshape(TOKENS_PER_SHARE, QUERY_HEADS * HEAD_SIZE).astype(jnp.bfloat16)
    attention = lax.map(one_block, jnp.arange(TOKEN_COUNT // TOKENS_PER_SHARE, dtype=jnp.int32))
    attention = attention.reshape(TOKEN_COUNT, QUERY_HEADS * HEAD_SIZE)
    return jnp.dot(attention, out_weight, preferred_element_type=jnp.float32).astype(jnp.bfloat16)
```

```python
import functools
import math

import jax
import jax.numpy as jnp
from jax import lax
from jax.experimental import pallas as pl
from jax.experimental.pallas import tpu as pltpu
from jax.sharding import PartitionSpec as P

HEAD_SIZE = 128
FIRST_WINDOW = 512
SECOND_WINDOW = 16
LOG2E = 1.4426950408889634
KC = 4
PIECES = 4

MESH = pl.DeviceIdType.MESH


def kernel(n, q_ref, k1_ref, v1_ref, k2_ref, v2_ref, w_hbm, out_ref,
           kv, valid, k2f, v2f, k2e, v2e, s_ref, att, w_vmem, sendb, recvb,
           z_send, y_send, c_send, kv_recv, e_send, e_recv, x_send, x_recv, w_sem):
    rows = q_ref.shape[0]
    heads = q_ref.shape[1] // HEAD_SIZE
    groups = k1_ref.shape[1] // HEAD_SIZE
    per_group = heads // groups
    reach = FIRST_WINDOW // rows
    total_rows = kv.shape[1]
    half = w_hbm.shape[1] // 2
    piece = half // PIECES
    tail = SECOND_WINDOW

    i = lax.axis_index("ctx")
    x = lax.axis_index("head")
    c = lax.rem(i, 2)
    y = lax.rem(lax.div(i, 2), 2)

    w_copies = []
    for part in range(2):
        col = pl.multiple_of((1 - x if part == 0 else x) * half, half)
        w_copies.append(pltpu.make_async_copy(
            w_hbm.at[:, pl.ds(col, half)], w_vmem.at[part], w_sem.at[part]))
        w_copies[-1].start()

    barrier = pltpu.get_barrier_semaphore()
    pl.semaphore_signal(barrier, inc=1, device_id={"head": 1 - x}, device_id_type=MESH)
    pl.semaphore_signal(barrier, inc=1, device_id={"ctx": i + 2 - 4 * y}, device_id_type=MESH)
    count = jnp.int32(2)
    for step in (1, -1, 4, -4, 8, -8):
        ok = (i + step < n) if step > 0 else (i + step >= 0)

        @pl.when(ok)
        def _():
            pl.semaphore_signal(barrier, inc=1, device_id={"ctx": i + step}, device_id_type=MESH)

        count = count + jnp.where(ok, 1, 0)

    for g in range(groups):
        lanes = slice(g * HEAD_SIZE, (g + 1) * HEAD_SIZE)
        kv[g, reach * rows:(reach + 1) * rows, :HEAD_SIZE] = k1_ref[:, lanes]
        kv[g, reach * rows:(reach + 1) * rows, HEAD_SIZE:] = v1_ref[:, lanes]
    pl.semaphore_wait(barrier, count)

    def slot(g, s):
        return kv.at[g, pl.ds(pl.multiple_of(s * rows, rows), rows)]

    def send(g, src, dst, send_sem, target):
        return pltpu.make_async_remote_copy(
            src_ref=slot(g, src), dst_ref=slot(g, dst), send_sem=send_sem,
            recv_sem=kv_recv.at[g, dst], device_id={"ctx": target}, device_id_type=MESH)

    def arrive(g, s):
        @pl.when(i >= reach - s)
        def _():
            pltpu.make_async_remote_copy(
                src_ref=slot(g, s), dst_ref=slot(g, s), send_sem=z_send.at[g, 0],
                recv_sem=kv_recv.at[g, s], device_id={"ctx": i + 1 - 2 * c}, device_id_type=MESH).wait_recv()

    z_list = [(4, 0), (8, 1)]

    def z_copy(g, step, idx):
        return send(g, reach, reach - step, z_send.at[g, idx], i + step)

    def y_copy(g, j):
        return send(g, reach - 4 * j - 4 * y, reach - 2 - 4 * j, y_send.at[g, j], i + 2 - 4 * y)

    def c_copy(g, j):
        return send(g, reach - 2 * j - 2 * c, reach - 1 - 2 * j, c_send.at[g, j], i + 1 - 2 * c)

    for g in range(groups):
        for step, idx in z_list:
            @pl.when(i + step < n)
            def _():
                z_copy(g, step, idx).start()

    def edge(src, dst, idx):
        return pltpu.make_async_remote_copy(
            src_ref=src.at[rows - tail:, :], dst_ref=dst, send_sem=e_send.at[idx],
            recv_sem=e_recv.at[idx], device_id={"ctx": i + 1}, device_id_type=MESH)

    @pl.when(i + 1 < n)
    def _():
        edge(k2_ref, k2e, 0).start()
        edge(v2_ref, v2e, 1).start()

    for g in range(groups):
        lanes = slice(g * HEAD_SIZE, (g + 1) * HEAD_SIZE)
        kv[g, (reach + 1) * rows:, :] = jnp.zeros((total_rows - (reach + 1) * rows, 2 * HEAD_SIZE), jnp.bfloat16)
        for s in range(reach):
            @pl.when(i < reach - s)
            def _():
                kv[g, s * rows:(s + 1) * rows, :HEAD_SIZE] = jnp.broadcast_to(
                    k1_ref[0:1, lanes], (rows, HEAD_SIZE))
                kv[g, s * rows:(s + 1) * rows, HEAD_SIZE:] = jnp.zeros((rows, HEAD_SIZE), jnp.bfloat16)
        k2f[g, tail:, :] = k2_ref[:, lanes].astype(jnp.float32)
        v2f[g, tail:, :HEAD_SIZE] = v2_ref[:, lanes].astype(jnp.float32)
        v2f[g, tail:, HEAD_SIZE:] = jnp.ones((rows, HEAD_SIZE), jnp.float32)
    row_id = lax.broadcasted_iota(jnp.int32, valid.shape, 0)
    exists = (row_id >= (reach - i) * rows) & (row_id < (reach + 1) * rows)
    valid[...] = jnp.where(exists, 1.0, 0.0).astype(jnp.bfloat16)

    def start_y(g):
        for j in range(2):
            @pl.when(i >= 4 * j + 4 * y)
            def _():
                y_copy(g, j).start()

    def start_c(g, parity):
        for j in range(4):
            @pl.when((i >= 2 * j + 2 * c) & (lax.rem(j + c, 2) == parity))
            def _():
                c_copy(g, j).start()

    for g in range(groups):
        arrive(g, reach - 4)
        arrive(g, reach - 8)
        start_y(g)
        start_c(g, 0)
    for g in range(groups):
        arrive(g, reach - 2)
        arrive(g, reach - 6)
        start_c(g, 1)

    @pl.when(i >= 1)
    def _():
        for idx, (src, dst) in enumerate(((k2_ref, k2e), (v2_ref, v2e))):
            edge(src, dst, idx).wait_recv()
        for g in range(groups):
            lanes = slice(g * HEAD_SIZE, (g + 1) * HEAD_SIZE)
            k2f[g, :tail, :] = k2e[:, lanes].astype(jnp.float32)
            v2f[g, :tail, :HEAD_SIZE] = v2e[:, lanes].astype(jnp.float32)
            v2f[g, :tail, HEAD_SIZE:] = jnp.ones((tail, HEAD_SIZE), jnp.float32)

    @pl.when(i < 1)
    def _():
        for g in range(groups):
            k2f[g, :tail, :] = jnp.broadcast_to(k2f[g, tail:tail + 1, :], (tail, HEAD_SIZE))
            v2f[g, :tail, :] = jnp.zeros((tail, 2 * HEAD_SIZE), jnp.float32)

    for g in range(groups):
        for s in range(reach - 1, 0, -2):
            arrive(g, s)

    lane = lax.broadcasted_iota(jnp.int32, (rows, HEAD_SIZE), 1)
    token = lax.broadcasted_iota(jnp.int32, (rows, HEAD_SIZE), 0)
    own = ((lane < rows) & (lane <= token))[None]
    scale = LOG2E / math.sqrt(HEAD_SIZE)
    span = KC * rows
    chunks = SECOND_WINDOW // KC

    def one_head(h, carry):
        g = lax.div(h, per_group)
        at = pl.ds(pl.multiple_of(h * HEAD_SIZE, HEAD_SIZE), HEAD_SIZE)
        query = q_ref[:, at].astype(jnp.float32) * scale
        keys = kv[g, :, :HEAD_SIZE]
        mixed = jnp.concatenate([kv[g, :, HEAD_SIZE:], valid[...]], axis=1)
        top = None
        for chunk in range(chunks):
            products = jnp.concatenate(
                [(query * k2f[g, k + 1:k + 1 + rows, :]).astype(jnp.bfloat16)
                 for k in range(chunk * KC, (chunk + 1) * KC)], axis=0)
            s = lax.dot_general(products, keys, (((1,), (1,)), ((), ())),
                                preferred_element_type=jnp.float32)
            s = s.reshape(KC, rows, total_rows)
            first = jnp.where(own, s[:, :, FIRST_WINDOW:], s[:, :, :HEAD_SIZE])
            rest = s[:, :, HEAD_SIZE:FIRST_WINDOW]
            s_ref[chunk * KC:(chunk + 1) * KC, :, :HEAD_SIZE] = first
            s_ref[chunk * KC:(chunk + 1) * KC, :, HEAD_SIZE:] = rest
            high = jnp.max(first, axis=0)
            for tile in range((FIRST_WINDOW - HEAD_SIZE) // HEAD_SIZE):
                high = jnp.maximum(high, jnp.max(rest[:, :, tile * HEAD_SIZE:(tile + 1) * HEAD_SIZE], axis=0))
            top = high if top is None else jnp.maximum(top, high)
        top = jnp.max(top, axis=1, keepdims=True)[None]
        acc = jnp.zeros((rows, 2 * HEAD_SIZE), jnp.float32)
        for chunk in range(chunks):
            e = jnp.exp2(s_ref[chunk * KC:(chunk + 1) * KC] - top)
            first = e[:, :, :HEAD_SIZE]
            weights = jnp.concatenate(
                [jnp.where(own, 0.0, first).astype(jnp.bfloat16), e[:, :, HEAD_SIZE:].astype(jnp.bfloat16),
                 jnp.where(own, first, 0.0).astype(jnp.bfloat16)], axis=2).reshape(span, total_rows)
            o = jnp.dot(weights, mixed, preferred_element_type=jnp.float32)
            for k in range(KC):
                acc = acc + o[k * rows:(k + 1) * rows] * v2f[g, pl.ds(chunk * KC + k + 1, rows), :]
        att[:, at] = (acc[:, :HEAD_SIZE] / acc[:, HEAD_SIZE:]).astype(jnp.bfloat16)
        return carry

    lax.fori_loop(0, heads, one_head, 0)

    def x_copy(p):
        return pltpu.make_async_remote_copy(
            src_ref=sendb.at[p], dst_ref=recvb.at[p], send_sem=x_send.at[p],
            recv_sem=x_recv.at[p], device_id={"head": 1 - x}, device_id_type=MESH)

    w_copies[0].wait()
    for p in range(PIECES):
        sendb[p] = jnp.dot(att[...], w_vmem[0, :, p * piece:(p + 1) * piece],
                           preferred_element_type=jnp.float32).astype(jnp.bfloat16)
        x_copy(p).start()
    w_copies[1].wait()
    for p in range(PIECES):
        mine = jnp.dot(att[...], w_vmem[1, :, p * piece:(p + 1) * piece],
                       preferred_element_type=jnp.float32)
        x_copy(p).wait_recv()
        out_ref[:, p * piece:(p + 1) * piece] = (mine + recvb[p].astype(jnp.float32)).astype(jnp.bfloat16)

    for p in range(PIECES):
        x_copy(p).wait_send()

    @pl.when(i + 1 < n)
    def _():
        edge(k2_ref, k2e, 0).wait_send()
        edge(v2_ref, v2e, 1).wait_send()

    for g in range(groups):
        for step, idx in z_list:
            @pl.when(i + step < n)
            def _():
                z_copy(g, step, idx).wait_send()
        for j in range(2):
            @pl.when(i >= 4 * j + 4 * y)
            def _():
                y_copy(g, j).wait_send()
        for j in range(4):
            @pl.when(i >= 2 * j + 2 * c)
            def _():
                c_copy(g, j).wait_send()


def body(n, queries, keys_first, primary_value_array, keys_second, secondary_value_array, out_weight):
    rows = queries.shape[0]
    groups = keys_first.shape[1] // HEAD_SIZE
    width = keys_first.shape[1]
    depth, features = out_weight.shape
    half = features // 2
    total_rows = FIRST_WINDOW + HEAD_SIZE
    vmem = pl.BlockSpec(memory_space=pltpu.VMEM)
    return pl.pallas_call(
        functools.partial(kernel, n),
        out_shape=jax.ShapeDtypeStruct((rows, half), jnp.bfloat16),
        in_specs=[vmem] * 5 + [pl.BlockSpec(memory_space=pl.ANY)],
        out_specs=vmem,
        scratch_shapes=[
            pltpu.VMEM((groups, total_rows, 2 * HEAD_SIZE), jnp.bfloat16),
            pltpu.VMEM((total_rows, HEAD_SIZE), jnp.bfloat16),
            pltpu.VMEM((groups, rows + SECOND_WINDOW, HEAD_SIZE), jnp.float32),
            pltpu.VMEM((groups, rows + SECOND_WINDOW, 2 * HEAD_SIZE), jnp.float32),
            pltpu.VMEM((SECOND_WINDOW, width), jnp.bfloat16),
            pltpu.VMEM((SECOND_WINDOW, width), jnp.bfloat16),
            pltpu.VMEM((SECOND_WINDOW, rows, FIRST_WINDOW), jnp.float32),
            pltpu.VMEM((rows, depth), jnp.bfloat16),
            pltpu.VMEM((2, depth, half), jnp.bfloat16),
            pltpu.VMEM((PIECES, rows, half // PIECES), jnp.bfloat16),
            pltpu.VMEM((PIECES, rows, half // PIECES), jnp.bfloat16),
            pltpu.SemaphoreType.DMA((groups, 2)),
            pltpu.SemaphoreType.DMA((groups, 2)),
            pltpu.SemaphoreType.DMA((groups, 4)),
            pltpu.SemaphoreType.DMA((groups, FIRST_WINDOW // rows)),
            pltpu.SemaphoreType.DMA((2,)),
            pltpu.SemaphoreType.DMA((2,)),
            pltpu.SemaphoreType.DMA((PIECES,)),
            pltpu.SemaphoreType.DMA((PIECES,)),
            pltpu.SemaphoreType.DMA((2,)),
        ],
        compiler_params=pltpu.CompilerParams(
            collective_id=0, has_side_effects=True, vmem_limit_bytes=48 * 1024 * 1024),
        cost_estimate=pl.CostEstimate(flops=3_000_000_000, bytes_accessed=9_000_000, transcendentals=4_200_000),
    )(queries, keys_first, primary_value_array, keys_second, secondary_value_array, out_weight)


def solution(mesh):
    in_specs = (
        P("ctx", "head"),
        P("ctx", "head"),
        P("ctx", "head"),
        P("ctx", "head"),
        P("ctx", "head"),
        P("head", None),
    )
    return jax.shard_map(functools.partial(body, mesh.shape["ctx"]), mesh=mesh, in_specs=in_specs,
                         out_specs=P("ctx", "head"), check_vma=False)
```

```python
import functools
import math

import jax
import jax.numpy as jnp
from jax import lax
from jax.experimental import pallas as pl
from jax.experimental.pallas import tpu as pltpu
from jax.sharding import PartitionSpec as P

HEAD_SIZE = 128
FIRST_WINDOW = 512
SECOND_WINDOW = 16
LOG2E = 1.4426950408889634
KC = 8
PIECES = 2
PARTS = 2

MESH = pl.DeviceIdType.MESH


def kernel(n, q_hbm, k1_hbm, v1_hbm, k2_hbm, v2_hbm, w_hbm, out_ref,
           q_ref, k2_ref, v2_ref, kv, valid, k2f, v2f, k2e, v2e, s_ref, att, w_vmem, sendb, recvb,
           z_send, y_send, c_send, kv_recv, e_send, e_recv, x_send, x_recv, w_sem, in_sem, own_sem):
    rows = q_ref.shape[0]
    heads = q_ref.shape[1] // HEAD_SIZE
    groups = k2_ref.shape[1] // HEAD_SIZE
    per_group = heads // groups
    reach = FIRST_WINDOW // rows
    total_rows = kv.shape[1]
    half = w_hbm.shape[1] // 2
    piece = half // PIECES
    tail = SECOND_WINDOW
    part_rows = rows // PARTS

    i = lax.axis_index("ctx")
    x = lax.axis_index("head")
    c = lax.rem(i, 2)
    y = lax.rem(lax.div(i, 2), 2)

    own_copies = []
    for g in range(groups):
        lanes = slice(g * HEAD_SIZE, (g + 1) * HEAD_SIZE)
        own_rows = slice(reach * rows, (reach + 1) * rows)
        own_copies.append([
            pltpu.make_async_copy(k1_hbm.at[:, lanes], kv.at[g, own_rows, :HEAD_SIZE], own_sem.at[g, 0]),
            pltpu.make_async_copy(v1_hbm.at[:, lanes], kv.at[g, own_rows, HEAD_SIZE:], own_sem.at[g, 1])])
        for copy in own_copies[-1]:
            copy.start()
    in_copies = [pltpu.make_async_copy(src, dst, in_sem.at[idx]) for idx, (src, dst) in enumerate(
        ((k2_hbm, k2_ref), (v2_hbm, v2_ref), (q_hbm, q_ref)))]
    for copy in in_copies:
        copy.start()
    w_copies = []
    for part in range(2):
        col = pl.multiple_of((1 - x if part == 0 else x) * half, half)
        w_copies.append(pltpu.make_async_copy(
            w_hbm.at[:, pl.ds(col, half)], w_vmem.at[part], w_sem.at[part]))

    barrier = pltpu.get_barrier_semaphore()
    pl.semaphore_signal(barrier, inc=1, device_id={"head": 1 - x}, device_id_type=MESH)
    pl.semaphore_signal(barrier, inc=1, device_id={"ctx": i + 2 - 4 * y}, device_id_type=MESH)
    count = jnp.int32(2)
    for step in (1, -1, 4, -4, 8, -8):
        ok = (i + step < n) if step > 0 else (i + step >= 0)

        @pl.when(ok)
        def _():
            pl.semaphore_signal(barrier, inc=1, device_id={"ctx": i + step}, device_id_type=MESH)

        count = count + jnp.where(ok, 1, 0)

    pl.semaphore_wait(barrier, count)

    def slot(g, s):
        return kv.at[g, pl.ds(pl.multiple_of(s * rows, rows), rows)]

    def send(g, src, dst, send_sem, target):
        return pltpu.make_async_remote_copy(
            src_ref=slot(g, src), dst_ref=slot(g, dst), send_sem=send_sem,
            recv_sem=kv_recv.at[g, dst], device_id={"ctx": target}, device_id_type=MESH)

    def arrive(g, s):
        @pl.when(i >= reach - s)
        def _():
            pltpu.make_async_remote_copy(
                src_ref=slot(g, s), dst_ref=slot(g, s), send_sem=z_send.at[g, 0],
                recv_sem=kv_recv.at[g, s], device_id={"ctx": i + 1 - 2 * c}, device_id_type=MESH).wait_recv()

    z_list = [(4, 0), (8, 1)]

    def z_copy(g, step, idx):
        return send(g, reach, reach - step, z_send.at[g, idx], i + step)

    def y_copy(g, j):
        return send(g, reach - 4 * j - 4 * y, reach - 2 - 4 * j, y_send.at[g, j], i + 2 - 4 * y)

    def c_copy(g, j):
        return send(g, reach - 2 * j - 2 * c, reach - 1 - 2 * j, c_send.at[g, j], i + 1 - 2 * c)

    for g in range(groups):
        for copy in own_copies[g]:
            copy.wait()
        for step, idx in z_list:
            @pl.when(i + step < n)
            def _():
                z_copy(g, step, idx).start()

    def edge(src, dst, idx):
        return pltpu.make_async_remote_copy(
            src_ref=src.at[rows - tail:, :], dst_ref=dst, send_sem=e_send.at[idx],
            recv_sem=e_recv.at[idx], device_id={"ctx": i + 1}, device_id_type=MESH)

    for copy in in_copies:
        copy.wait()

    @pl.when(i + 1 < n)
    def _():
        edge(k2_ref, k2e, 0).start()
        edge(v2_ref, v2e, 1).start()

    for g in range(groups):
        lanes = slice(g * HEAD_SIZE, (g + 1) * HEAD_SIZE)
        kv[g, (reach + 1) * rows:, :] = jnp.zeros((total_rows - (reach + 1) * rows, 2 * HEAD_SIZE), jnp.bfloat16)
        for s in range(reach):
            @pl.when(i < reach - s)
            def _():
                kv[g, s * rows:(s + 1) * rows, :HEAD_SIZE] = jnp.broadcast_to(
                    kv[g, reach * rows:reach * rows + 1, :HEAD_SIZE], (rows, HEAD_SIZE))
                kv[g, s * rows:(s + 1) * rows, HEAD_SIZE:] = jnp.zeros((rows, HEAD_SIZE), jnp.bfloat16)
        k2f[g, tail:, :] = k2_ref[:, lanes].astype(jnp.float32)
        v2f[g, tail:, :HEAD_SIZE] = v2_ref[:, lanes].astype(jnp.float32)
        v2f[g, tail:, HEAD_SIZE:] = jnp.ones((rows, HEAD_SIZE), jnp.float32)
    row_id = lax.broadcasted_iota(jnp.int32, valid.shape, 0)
    exists = (row_id >= (reach - i) * rows) & (row_id < (reach + 1) * rows)
    valid[...] = jnp.where(exists, 1.0, 0.0).astype(jnp.bfloat16)

    def start_y(g):
        for j in range(2):
            @pl.when(i >= 4 * j + 4 * y)
            def _():
                y_copy(g, j).start()

    def start_c(g, parity):
        for j in range(4):
            @pl.when((i >= 2 * j + 2 * c) & (lax.rem(j + c, 2) == parity))
            def _():
                c_copy(g, j).start()

    def second_stage(g):
        arrive(g, reach - 4)
        arrive(g, reach - 8)
        start_y(g)
        start_c(g, 0)

    def third_stage(g):
        arrive(g, reach - 2)
        arrive(g, reach - 6)
        start_c(g, 1)

    def last_stage(g):
        for s in range(reach - 1, 0, -2):
            arrive(g, s)

    second_stage(0)
    third_stage(0)

    @pl.when(i >= 1)
    def _():
        for idx, (src, dst) in enumerate(((k2_ref, k2e), (v2_ref, v2e))):
            edge(src, dst, idx).wait_recv()
        for g in range(groups):
            lanes = slice(g * HEAD_SIZE, (g + 1) * HEAD_SIZE)
            k2f[g, :tail, :] = k2e[:, lanes].astype(jnp.float32)
            v2f[g, :tail, :HEAD_SIZE] = v2e[:, lanes].astype(jnp.float32)
            v2f[g, :tail, HEAD_SIZE:] = jnp.ones((tail, HEAD_SIZE), jnp.float32)

    @pl.when(i < 1)
    def _():
        for g in range(groups):
            k2f[g, :tail, :] = jnp.broadcast_to(k2f[g, tail:tail + 1, :], (tail, HEAD_SIZE))
            v2f[g, :tail, :] = jnp.zeros((tail, 2 * HEAD_SIZE), jnp.float32)

    for g in range(1, groups):
        second_stage(g)
    for copy in w_copies:
        copy.start()
    last_stage(0)

    lane = lax.broadcasted_iota(jnp.int32, (part_rows, HEAD_SIZE), 1)
    token = lax.broadcasted_iota(jnp.int32, (part_rows, HEAD_SIZE), 0)
    scale = LOG2E / math.sqrt(HEAD_SIZE)
    span = KC * part_rows
    chunks = SECOND_WINDOW // KC

    def attend(g, part):
        start = part * part_rows
        own = ((lane < rows) & (lane <= token + start))[None]

        def one_head(member, carry):
            at = pl.ds(pl.multiple_of((g * per_group + member) * HEAD_SIZE, HEAD_SIZE), HEAD_SIZE)
            query = q_ref[start:start + part_rows, at].astype(jnp.float32) * scale
            keys = kv[g, :, :HEAD_SIZE]
            mixed = jnp.concatenate([kv[g, :, HEAD_SIZE:], valid[...]], axis=1)
            top = None
            for chunk in range(chunks):
                products = jnp.concatenate(
                    [(query * k2f[g, start + k + 1:start + k + 1 + part_rows, :]).astype(jnp.bfloat16)
                     for k in range(chunk * KC, (chunk + 1) * KC)], axis=0)
                s = lax.dot_general(products, keys, (((1,), (1,)), ((), ())),
                                    preferred_element_type=jnp.float32)
                s = s.reshape(KC, part_rows, total_rows)
                first = jnp.where(own, s[:, :, FIRST_WINDOW:], s[:, :, :HEAD_SIZE])
                rest = s[:, :, HEAD_SIZE:FIRST_WINDOW]
                s_ref[chunk * KC:(chunk + 1) * KC, :, :HEAD_SIZE] = first
                s_ref[chunk * KC:(chunk + 1) * KC, :, HEAD_SIZE:] = rest
                high = jnp.max(first, axis=0)
                for tile in range((FIRST_WINDOW - HEAD_SIZE) // HEAD_SIZE):
                    high = jnp.maximum(high, jnp.max(rest[:, :, tile * HEAD_SIZE:(tile + 1) * HEAD_SIZE], axis=0))
                top = high if top is None else jnp.maximum(top, high)
            top = jnp.max(top, axis=1, keepdims=True)[None]
            acc = jnp.zeros((part_rows, 2 * HEAD_SIZE), jnp.float32)
            for chunk in range(chunks):
                e = jnp.exp2(s_ref[chunk * KC:(chunk + 1) * KC] - top)
                first = e[:, :, :HEAD_SIZE]
                weights = jnp.concatenate(
                    [jnp.where(own, 0.0, first).astype(jnp.bfloat16), e[:, :, HEAD_SIZE:].astype(jnp.bfloat16),
                     jnp.where(own, first, 0.0).astype(jnp.bfloat16)], axis=2).reshape(span, total_rows)
                o = jnp.dot(weights, mixed, preferred_element_type=jnp.float32)
                for k in range(KC):
                    second = start + chunk * KC + k + 1
                    acc = acc + o[k * part_rows:(k + 1) * part_rows] * v2f[g, second:second + part_rows, :]
            att[start:start + part_rows, at] = (acc[:, :HEAD_SIZE] / acc[:, HEAD_SIZE:]).astype(jnp.bfloat16)
            return carry

        lax.fori_loop(0, per_group, one_head, 0, unroll=2)

    def x_copy(part, p):
        return pltpu.make_async_remote_copy(
            src_ref=sendb.at[part, p], dst_ref=recvb.at[part, p], send_sem=x_send.at[part, p],
            recv_sem=x_recv.at[part, p], device_id={"head": 1 - x}, device_id_type=MESH)

    def project(part):
        for p in range(PIECES):
            sendb[part, p] = jnp.dot(
                att[part * part_rows:(part + 1) * part_rows, :], w_vmem[0, :, p * piece:(p + 1) * piece],
                preferred_element_type=jnp.float32).astype(jnp.bfloat16)
            x_copy(part, p).start()

    for g in range(groups):
        for part in range(PARTS):
            attend(g, part)
            if g == 0 and part == 0:
                for later in range(1, groups):
                    third_stage(later)
            if part == PARTS - 1 and g < groups - 1:
                last_stage(g + 1)
            if g == groups - 1:
                if part == 0:
                    w_copies[0].wait()
                project(part)
    w_copies[1].wait()
    for p in range(PIECES):
        mine = jnp.dot(att[...], w_vmem[1, :, p * piece:(p + 1) * piece],
                       preferred_element_type=jnp.float32)
        for part in range(PARTS):
            x_copy(part, p).wait_recv()
            at = slice(part * part_rows, (part + 1) * part_rows)
            out_ref[at, p * piece:(p + 1) * piece] = (
                mine[at] + recvb[part, p].astype(jnp.float32)).astype(jnp.bfloat16)

    for part in range(PARTS):
        for p in range(PIECES):
            x_copy(part, p).wait_send()

    @pl.when(i + 1 < n)
    def _():
        edge(k2_ref, k2e, 0).wait_send()
        edge(v2_ref, v2e, 1).wait_send()

    for g in range(groups):
        for step, idx in z_list:
            @pl.when(i + step < n)
            def _():
                z_copy(g, step, idx).wait_send()
        for j in range(2):
            @pl.when(i >= 4 * j + 4 * y)
            def _():
                y_copy(g, j).wait_send()
        for j in range(4):
            @pl.when(i >= 2 * j + 2 * c)
            def _():
                c_copy(g, j).wait_send()


def body(n, queries, keys_first, primary_value_array, keys_second, secondary_value_array, out_weight):
    rows = queries.shape[0]
    groups = keys_first.shape[1] // HEAD_SIZE
    width = keys_first.shape[1]
    depth, features = out_weight.shape
    half = features // 2
    total_rows = FIRST_WINDOW + HEAD_SIZE
    vmem = pl.BlockSpec(memory_space=pltpu.VMEM)
    return pl.pallas_call(
        functools.partial(kernel, n),
        out_shape=jax.ShapeDtypeStruct((rows, half), jnp.bfloat16),
        in_specs=[pl.BlockSpec(memory_space=pltpu.HBM)] * 6,
        out_specs=vmem,
        scratch_shapes=[
            pltpu.VMEM(queries.shape, jnp.bfloat16),
            pltpu.VMEM(keys_second.shape, jnp.bfloat16),
            pltpu.VMEM(keys_second.shape, jnp.bfloat16),
            pltpu.VMEM((groups, total_rows, 2 * HEAD_SIZE), jnp.bfloat16),
            pltpu.VMEM((total_rows, HEAD_SIZE), jnp.bfloat16),
            pltpu.VMEM((groups, rows + SECOND_WINDOW, HEAD_SIZE), jnp.float32),
            pltpu.VMEM((groups, rows + SECOND_WINDOW, 2 * HEAD_SIZE), jnp.float32),
            pltpu.VMEM((SECOND_WINDOW, width), jnp.bfloat16),
            pltpu.VMEM((SECOND_WINDOW, width), jnp.bfloat16),
            pltpu.VMEM((SECOND_WINDOW, rows // PARTS, FIRST_WINDOW), jnp.float32),
            pltpu.VMEM((rows, depth), jnp.bfloat16),
            pltpu.VMEM((2, depth, half), jnp.bfloat16),
            pltpu.VMEM((PARTS, PIECES, rows // PARTS, half // PIECES), jnp.bfloat16),
            pltpu.VMEM((PARTS, PIECES, rows // PARTS, half // PIECES), jnp.bfloat16),
            pltpu.SemaphoreType.DMA((groups, 2)),
            pltpu.SemaphoreType.DMA((groups, 2)),
            pltpu.SemaphoreType.DMA((groups, 4)),
            pltpu.SemaphoreType.DMA((groups, FIRST_WINDOW // rows)),
            pltpu.SemaphoreType.DMA((2,)),
            pltpu.SemaphoreType.DMA((2,)),
            pltpu.SemaphoreType.DMA((PARTS, PIECES)),
            pltpu.SemaphoreType.DMA((PARTS, PIECES)),
            pltpu.SemaphoreType.DMA((2,)),
            pltpu.SemaphoreType.DMA((3,)),
            pltpu.SemaphoreType.DMA((groups, 2)),
        ],
        compiler_params=pltpu.CompilerParams(
            collective_id=0, has_side_effects=True, vmem_limit_bytes=64 * 1024 * 1024 - 65536),
        cost_estimate=pl.CostEstimate(flops=3_000_000_000, bytes_accessed=9_000_000, transcendentals=4_200_000),
    )(queries, keys_first, primary_value_array, keys_second, secondary_value_array, out_weight)


def solution(mesh):
    in_specs = (
        P("ctx", "head"),
        P("ctx", "head"),
        P("ctx", "head"),
        P("ctx", "head"),
        P("ctx", "head"),
        P("head", None),
    )
    return jax.shard_map(functools.partial(body, mesh.shape["ctx"]), mesh=mesh, in_specs=in_specs,
                         out_specs=P("ctx", "head"), check_vma=False)
```

```python
import functools
import math

import jax
import jax.numpy as jnp
from jax import lax
from jax.experimental import pallas as pl
from jax.experimental.pallas import tpu as pltpu
from jax.sharding import PartitionSpec as P

HEAD_SIZE = 128
FIRST_WINDOW = 512
SECOND_WINDOW = 16
LOG2E = 1.4426950408889634
KC = 16
PIECES = 2
PARTS = 2

MESH = pl.DeviceIdType.MESH


def kernel(n, q_hbm, k1_hbm, v1_hbm, k2_hbm, v2_hbm, w_hbm, out_ref,
           q_ref, k2_ref, v2_ref, kv, valid, k2f, v2f, k2e, v2e, s_ref, att, w_vmem, sendb, recvb,
           z_send, y_send, c_send, kv_recv, e_send, e_recv, x_send, x_recv, w_sem, in_sem, own_sem):
    rows = q_ref.shape[0]
    heads = q_ref.shape[1] // HEAD_SIZE
    groups = k2_ref.shape[1] // HEAD_SIZE
    per_group = heads // groups
    reach = FIRST_WINDOW // rows
    total_rows = kv.shape[1]
    half = w_hbm.shape[1] // 2
    piece = half // PIECES
    tail = SECOND_WINDOW
    part_rows = rows // PARTS

    i = lax.axis_index("ctx")
    x = lax.axis_index("head")
    c = lax.rem(i, 2)
    y = lax.rem(lax.div(i, 2), 2)

    own_copies = []
    for g in range(groups):
        lanes = slice(g * HEAD_SIZE, (g + 1) * HEAD_SIZE)
        own_rows = slice(reach * rows, (reach + 1) * rows)
        own_copies.append([
            pltpu.make_async_copy(k1_hbm.at[:, lanes], kv.at[g, own_rows, :HEAD_SIZE], own_sem.at[g, 0]),
            pltpu.make_async_copy(v1_hbm.at[:, lanes], kv.at[g, own_rows, HEAD_SIZE:], own_sem.at[g, 1])])
        for copy in own_copies[-1]:
            copy.start()
    in_copies = [pltpu.make_async_copy(src, dst, in_sem.at[idx]) for idx, (src, dst) in enumerate(
        ((k2_hbm, k2_ref), (v2_hbm, v2_ref), (q_hbm, q_ref)))]
    for copy in in_copies:
        copy.start()
    w_copies = []
    for part in range(2):
        col = pl.multiple_of((1 - x if part == 0 else x) * half, half)
        w_copies.append(pltpu.make_async_copy(
            w_hbm.at[:, pl.ds(col, half)], w_vmem.at[part], w_sem.at[part]))

    barrier = pltpu.get_barrier_semaphore()
    pl.semaphore_signal(barrier, inc=1, device_id={"head": 1 - x}, device_id_type=MESH)
    pl.semaphore_signal(barrier, inc=1, device_id={"ctx": i + 2 - 4 * y}, device_id_type=MESH)
    count = jnp.int32(2)
    for step in (1, -1, 4, -4, 8, -8):
        ok = (i + step < n) if step > 0 else (i + step >= 0)

        @pl.when(ok)
        def _():
            pl.semaphore_signal(barrier, inc=1, device_id={"ctx": i + step}, device_id_type=MESH)

        count = count + jnp.where(ok, 1, 0)

    pl.semaphore_wait(barrier, count)

    def slot(g, s):
        return kv.at[g, pl.ds(pl.multiple_of(s * rows, rows), rows)]

    def send(g, src, dst, send_sem, target):
        return pltpu.make_async_remote_copy(
            src_ref=slot(g, src), dst_ref=slot(g, dst), send_sem=send_sem,
            recv_sem=kv_recv.at[g, dst], device_id={"ctx": target}, device_id_type=MESH)

    def arrive(g, s):
        @pl.when(i >= reach - s)
        def _():
            pltpu.make_async_remote_copy(
                src_ref=slot(g, s), dst_ref=slot(g, s), send_sem=z_send.at[g, 0],
                recv_sem=kv_recv.at[g, s], device_id={"ctx": i + 1 - 2 * c}, device_id_type=MESH).wait_recv()

    z_list = [(4, 0), (8, 1)]

    def z_copy(g, step, idx):
        return send(g, reach, reach - step, z_send.at[g, idx], i + step)

    def y_copy(g, j):
        return send(g, reach - 4 * j - 4 * y, reach - 2 - 4 * j, y_send.at[g, j], i + 2 - 4 * y)

    def c_copy(g, j):
        return send(g, reach - 2 * j - 2 * c, reach - 1 - 2 * j, c_send.at[g, j], i + 1 - 2 * c)

    def forward(g, back):
        for j in range(2):
            if back % 4 == 0 and 0 <= back // 4 - j <= 1:
                @pl.when((i >= back) & (y == back // 4 - j))
                def _():
                    y_copy(g, j).start()
        for j in range(4):
            if 0 <= back // 2 - j <= 1:
                @pl.when((i >= back) & (c == back // 2 - j))
                def _():
                    c_copy(g, j).start()

    def first_stage(g):
        for step, idx in z_list:
            @pl.when(i + step < n)
            def _():
                z_copy(g, step, idx).start()
        forward(g, 0)

    for copies in own_copies:
        for copy in copies:
            copy.wait()
    first_stage(0)

    def edge(src, dst, idx):
        return pltpu.make_async_remote_copy(
            src_ref=src.at[rows - tail:, :], dst_ref=dst, send_sem=e_send.at[idx],
            recv_sem=e_recv.at[idx], device_id={"ctx": i + 1}, device_id_type=MESH)

    for copy in in_copies:
        copy.wait()

    @pl.when(i + 1 < n)
    def _():
        edge(k2_ref, k2e, 0).start()
        edge(v2_ref, v2e, 1).start()

    for g in range(groups):
        lanes = slice(g * HEAD_SIZE, (g + 1) * HEAD_SIZE)
        kv[g, (reach + 1) * rows:, :] = jnp.zeros((total_rows - (reach + 1) * rows, 2 * HEAD_SIZE), jnp.bfloat16)
        for s in range(reach):
            @pl.when(i < reach - s)
            def _():
                kv[g, s * rows:(s + 1) * rows, :HEAD_SIZE] = jnp.broadcast_to(
                    kv[g, reach * rows:reach * rows + 1, :HEAD_SIZE], (rows, HEAD_SIZE))
                kv[g, s * rows:(s + 1) * rows, HEAD_SIZE:] = jnp.zeros((rows, HEAD_SIZE), jnp.bfloat16)
        k2f[g, tail:, :] = k2_ref[:, lanes].astype(jnp.float32)
        v2f[g, tail:, :HEAD_SIZE] = v2_ref[:, lanes].astype(jnp.float32)
        v2f[g, tail:, HEAD_SIZE:] = jnp.ones((rows, HEAD_SIZE), jnp.float32)
    row_id = lax.broadcasted_iota(jnp.int32, valid.shape, 0)
    exists = (row_id >= (reach - i) * rows) & (row_id < (reach + 1) * rows)
    valid[...] = jnp.where(exists, 1.0, 0.0).astype(jnp.bfloat16)

    def second_stage(g):
        arrive(g, reach - 4)
        forward(g, 4)
        arrive(g, reach - 8)
        forward(g, 8)

    def third_stage(g):
        arrive(g, reach - 2)
        forward(g, 2)
        arrive(g, reach - 6)
        forward(g, 6)

    def last_stage(g):
        for s in range(reach - 1, 0, -2):
            arrive(g, s)

    second_stage(0)
    for g in range(1, groups):
        first_stage(g)
    third_stage(0)

    @pl.when(i >= 1)
    def _():
        for idx, (src, dst) in enumerate(((k2_ref, k2e), (v2_ref, v2e))):
            edge(src, dst, idx).wait_recv()
        for g in range(groups):
            lanes = slice(g * HEAD_SIZE, (g + 1) * HEAD_SIZE)
            k2f[g, :tail, :] = k2e[:, lanes].astype(jnp.float32)
            v2f[g, :tail, :HEAD_SIZE] = v2e[:, lanes].astype(jnp.float32)
            v2f[g, :tail, HEAD_SIZE:] = jnp.ones((tail, HEAD_SIZE), jnp.float32)

    @pl.when(i < 1)
    def _():
        for g in range(groups):
            k2f[g, :tail, :] = jnp.broadcast_to(k2f[g, tail:tail + 1, :], (tail, HEAD_SIZE))
            v2f[g, :tail, :] = jnp.zeros((tail, 2 * HEAD_SIZE), jnp.float32)

    for copy in w_copies:
        copy.start()
    last_stage(0)
    for g in range(1, groups):
        second_stage(g)

    lane = lax.broadcasted_iota(jnp.int32, (part_rows, HEAD_SIZE), 1)
    token = lax.broadcasted_iota(jnp.int32, (part_rows, HEAD_SIZE), 0)
    scale = LOG2E / math.sqrt(HEAD_SIZE)
    span = KC * part_rows
    chunks = SECOND_WINDOW // KC

    def attend(g, part):
        start = part * part_rows
        own = ((lane < rows) & (lane <= token + start))[None]

        def one_head(member, carry):
            at = pl.ds(pl.multiple_of((g * per_group + member) * HEAD_SIZE, HEAD_SIZE), HEAD_SIZE)
            query = q_ref[start:start + part_rows, at].astype(jnp.float32) * scale
            keys = kv[g, :, :HEAD_SIZE]
            mixed = jnp.concatenate([kv[g, :, HEAD_SIZE:], valid[...]], axis=1)
            top = None
            for chunk in range(chunks):
                products = jnp.concatenate(
                    [(query * k2f[g, start + k + 1:start + k + 1 + part_rows, :]).astype(jnp.bfloat16)
                     for k in range(chunk * KC, (chunk + 1) * KC)], axis=0)
                s = lax.dot_general(products, keys, (((1,), (1,)), ((), ())),
                                    preferred_element_type=jnp.float32)
                s = s.reshape(KC, part_rows, total_rows)
                first = jnp.where(own, s[:, :, FIRST_WINDOW:], s[:, :, :HEAD_SIZE])
                rest = s[:, :, HEAD_SIZE:FIRST_WINDOW]
                s_ref[chunk * KC:(chunk + 1) * KC, :, :HEAD_SIZE] = first
                s_ref[chunk * KC:(chunk + 1) * KC, :, HEAD_SIZE:] = rest
                high = jnp.max(first, axis=0)
                for tile in range((FIRST_WINDOW - HEAD_SIZE) // HEAD_SIZE):
                    high = jnp.maximum(high, jnp.max(rest[:, :, tile * HEAD_SIZE:(tile + 1) * HEAD_SIZE], axis=0))
                top = high if top is None else jnp.maximum(top, high)
            top = jnp.max(top, axis=1, keepdims=True)[None]
            acc = jnp.zeros((part_rows, 2 * HEAD_SIZE), jnp.float32)
            for chunk in range(chunks):
                e = jnp.exp2(s_ref[chunk * KC:(chunk + 1) * KC] - top)
                first = e[:, :, :HEAD_SIZE]
                weights = jnp.concatenate(
                    [jnp.where(own, 0.0, first).astype(jnp.bfloat16), e[:, :, HEAD_SIZE:].astype(jnp.bfloat16),
                     jnp.where(own, first, 0.0).astype(jnp.bfloat16)], axis=2).reshape(span, total_rows)
                o = jnp.dot(weights, mixed, preferred_element_type=jnp.float32)
                for k in range(KC):
                    second = start + chunk * KC + k + 1
                    acc = acc + o[k * part_rows:(k + 1) * part_rows] * v2f[g, second:second + part_rows, :]
            att[start:start + part_rows, at] = (acc[:, :HEAD_SIZE] / acc[:, HEAD_SIZE:]).astype(jnp.bfloat16)
            return carry

        lax.fori_loop(0, per_group, one_head, 0, unroll=4)

    def x_copy(part, p):
        return pltpu.make_async_remote_copy(
            src_ref=sendb.at[part, p], dst_ref=recvb.at[part, p], send_sem=x_send.at[part, p],
            recv_sem=x_recv.at[part, p], device_id={"head": 1 - x}, device_id_type=MESH)

    def project(part):
        for p in range(PIECES):
            sendb[part, p] = jnp.dot(
                att[part * part_rows:(part + 1) * part_rows, :], w_vmem[0, :, p * piece:(p + 1) * piece],
                preferred_element_type=jnp.float32).astype(jnp.bfloat16)
            x_copy(part, p).start()

    for g in range(groups):
        for part in range(PARTS):
            attend(g, part)
            if g == 0 and part == 0:
                for later in range(1, groups):
                    third_stage(later)
            if part == PARTS - 1 and g < groups - 1:
                last_stage(g + 1)
            if g == groups - 1:
                if part == 0:
                    w_copies[0].wait()
                project(part)
    w_copies[1].wait()
    for p in range(PIECES):
        mine = jnp.dot(att[...], w_vmem[1, :, p * piece:(p + 1) * piece],
                       preferred_element_type=jnp.float32)
        for part in range(PARTS):
            x_copy(part, p).wait_recv()
            at = slice(part * part_rows, (part + 1) * part_rows)
            out_ref[at, p * piece:(p + 1) * piece] = (
                mine[at] + recvb[part, p].astype(jnp.float32)).astype(jnp.bfloat16)

    for part in range(PARTS):
        for p in range(PIECES):
            x_copy(part, p).wait_send()

    @pl.when(i + 1 < n)
    def _():
        edge(k2_ref, k2e, 0).wait_send()
        edge(v2_ref, v2e, 1).wait_send()

    for g in range(groups):
        for step, idx in z_list:
            @pl.when(i + step < n)
            def _():
                z_copy(g, step, idx).wait_send()
        for j in range(2):
            @pl.when(i >= 4 * j + 4 * y)
            def _():
                y_copy(g, j).wait_send()
        for j in range(4):
            @pl.when(i >= 2 * j + 2 * c)
            def _():
                c_copy(g, j).wait_send()


def body(n, queries, keys_first, primary_value_array, keys_second, secondary_value_array, out_weight):
    rows = queries.shape[0]
    groups = keys_first.shape[1] // HEAD_SIZE
    width = keys_first.shape[1]
    depth, features = out_weight.shape
    half = features // 2
    total_rows = FIRST_WINDOW + HEAD_SIZE
    vmem = pl.BlockSpec(memory_space=pltpu.VMEM)
    return pl.pallas_call(
        functools.partial(kernel, n),
        out_shape=jax.ShapeDtypeStruct((rows, half), jnp.bfloat16),
        in_specs=[pl.BlockSpec(memory_space=pltpu.HBM)] * 6,
        out_specs=vmem,
        scratch_shapes=[
            pltpu.VMEM(queries.shape, jnp.bfloat16),
            pltpu.VMEM(keys_second.shape, jnp.bfloat16),
            pltpu.VMEM(keys_second.shape, jnp.bfloat16),
            pltpu.VMEM((groups, total_rows, 2 * HEAD_SIZE), jnp.bfloat16),
            pltpu.VMEM((total_rows, HEAD_SIZE), jnp.bfloat16),
            pltpu.VMEM((groups, rows + SECOND_WINDOW, HEAD_SIZE), jnp.float32),
            pltpu.VMEM((groups, rows + SECOND_WINDOW, 2 * HEAD_SIZE), jnp.float32),
            pltpu.VMEM((SECOND_WINDOW, width), jnp.bfloat16),
            pltpu.VMEM((SECOND_WINDOW, width), jnp.bfloat16),
            pltpu.VMEM((SECOND_WINDOW, rows // PARTS, FIRST_WINDOW), jnp.float32),
            pltpu.VMEM((rows, depth), jnp.bfloat16),
            pltpu.VMEM((2, depth, half), jnp.bfloat16),
            pltpu.VMEM((PARTS, PIECES, rows // PARTS, half // PIECES), jnp.bfloat16),
            pltpu.VMEM((PARTS, PIECES, rows // PARTS, half // PIECES), jnp.bfloat16),
            pltpu.SemaphoreType.DMA((groups, 2)),
            pltpu.SemaphoreType.DMA((groups, 2)),
            pltpu.SemaphoreType.DMA((groups, 4)),
            pltpu.SemaphoreType.DMA((groups, FIRST_WINDOW // rows)),
            pltpu.SemaphoreType.DMA((2,)),
            pltpu.SemaphoreType.DMA((2,)),
            pltpu.SemaphoreType.DMA((PARTS, PIECES)),
            pltpu.SemaphoreType.DMA((PARTS, PIECES)),
            pltpu.SemaphoreType.DMA((2,)),
            pltpu.SemaphoreType.DMA((3,)),
            pltpu.SemaphoreType.DMA((groups, 2)),
        ],
        compiler_params=pltpu.CompilerParams(
            collective_id=0, has_side_effects=True, vmem_limit_bytes=64 * 1024 * 1024 - 65536),
        cost_estimate=pl.CostEstimate(flops=3_000_000_000, bytes_accessed=9_000_000, transcendentals=4_200_000),
    )(queries, keys_first, primary_value_array, keys_second, secondary_value_array, out_weight)


def solution(mesh):
    in_specs = (
        P("ctx", "head"),
        P("ctx", "head"),
        P("ctx", "head"),
        P("ctx", "head"),
        P("ctx", "head"),
        P("head", None),
    )
    return jax.shard_map(functools.partial(body, mesh.shape["ctx"]), mesh=mesh, in_specs=in_specs,
                         out_specs=P("ctx", "head"), check_vma=False)
```
